256 devices in a mesh: sub: 64 (over y, z, core), grp: 4 (over x).
Axes of the slice: x: 4, y: 4, z: 8, core: 2. Of those that a mesh axis runs over, the one named last changes fastest.
Arguments:
- schur: bfloat16 [512, 1536, 1536], P(('sub', 'grp')), as said below
- local_gap: float32 [512, 1536, 128], P(('sub', 'grp')), may hold values from -6 to 6
- modes: float32 [512, 6, 1536], P(('sub', 'grp')), may hold values from -0.45927933 to 0.45927933
- rigid_loads: float32 [512, 6, 128], P(('sub', 'grp')), may hold values from -6 to 6
- coarse_inverse: float32 [3072, 3072], P(('sub', 'grp')), as said below
- block_slot: int32 [512, 12], P(('sub', 'grp')), may hold values from 0 to 11, each once within a row
- face_swap: int32 [512, 6], P(('sub', 'grp')), may hold values from 0 to 1, as said below
- lengths: int32 [512, 12], P(('sub', 'grp')), may hold values from 0 to 128, as said below
Outputs:
- multipliers: float32 [512, 1536, 128], P(('sub', 'grp'))
- residual_ratio: float32 [128], replicated
The draws below stay inside these ranges and needn't reach their ends.
Inputs may be any that keep to these rules, and one draw needn't show every extreme that they name: `schur`: each schur_s is symmetric positive definite. coarse_inverse is symmetric with a positive diagonal and small off-diagonal entries. `face_swap`: two subdomains that share a face hold the same value for it; absent faces hold any value. A slot and its partner slot have equal lengths; slots of absent faces have length 0; on every face toward a neighbour along sub one copy has length 128.
All inputs are finite; a program needn't handle non-finite values.
Results may differ from the reference program's by a relative error of at most 0.00075.
Values sent between devices are 32-bit elements; how exact they have to be, the bound alone decides.
No kernel may reach another device: no remote copies, remote signals or barrier semaphores. Data moves between devices by JAX's collectives and lax.ppermute only.
A program may use at most 128 MiB of HBM per device.

```python
import math
import jax
import jax.numpy as jnp
from jax import lax

BLK = 128
NB = 1536
BLOCKS = 12
MODES = 6
ITERS = 2
SUB_DEV = 2
NRHS = 128
CYCLE_STEP = 8
SUBDOMAINS = 512
COARSE = 3072
N_SUB = 64
N_GRP = 4


def face_tables(key):
    numbers = jnp.arange(SUBDOMAINS, dtype=jnp.int32)
    local_index = numbers % SUB_DEV
    group_index = numbers % CYCLE_STEP
    swap_plus = jax.random.randint(jax.random.fold_in(key, 21), (SUBDOMAINS, 3), 0, 2)
    span_plus = jax.random.randint(jax.random.fold_in(key, 22), (SUBDOMAINS, 3, 2), BLK // 4, BLK + 1)
    span_plus = span_plus.at[:, 2, 0].set(BLK)
    has_upper = jnp.stack([local_index < SUB_DEV - 1, group_index < CYCLE_STEP - SUB_DEV, numbers >= 0], axis=1).astype(jnp.int32)
    has_lower = jnp.stack([local_index > 0, group_index >= SUB_DEV, numbers >= 0], axis=1).astype(jnp.int32)
    strides = [1, SUB_DEV, CYCLE_STEP]
    swaps = []
    spans = []
    own_copy = jnp.arange(2, dtype=jnp.int32)
    for axis_number in range(3):
        below = (numbers - strides[axis_number]) % SUBDOMAINS
        lower_swap = swap_plus[below, axis_number]
        lower_span = span_plus[below[:, None], axis_number, (own_copy[None, :] + lower_swap[:, None]) % 2]
        lower_span = lower_span * has_lower[:, axis_number:axis_number + 1]
        upper_span = span_plus[:, axis_number, :] * has_upper[:, axis_number:axis_number + 1]
        swaps += [lower_swap, swap_plus[:, axis_number]]
        spans += [lower_span, upper_span]
    return (jnp.stack(swaps, axis=1).astype(jnp.int32), jnp.concatenate(spans, axis=1).astype(jnp.int32))


def draw_face_swap(key, part):
    return face_tables(key)[0]


def draw_lengths(key, part):
    return face_tables(key)[1]


def draw_schur(key, part):
    key = jax.random.fold_in(key, 3)

    def single(index):
        first_key, second_key = jax.random.split(jax.random.fold_in(key, index))
        noise = jax.random.normal(first_key, (NB, NB), jnp.float32)
        lower, upper = (0.7, 1.4)
        rough = jnp.exp(jax.random.uniform(second_key, (NB,), jnp.float32, math.log(lower), math.log(upper)))
        inner = jnp.eye(NB, dtype=jnp.float32) + 0.35 / math.sqrt(2.0 * NB) * (noise + noise.T)
        return (rough[:, None] * inner * rough[None, :]).astype(jnp.bfloat16)
    return lax.map(single, jnp.arange(SUBDOMAINS, dtype=jnp.int32))


def draw_coarse_inverse(key, part):
    key = jax.random.fold_in(key, 5)
    first_key, second_key = jax.random.split(key)
    noise = jax.random.normal(first_key, (COARSE, COARSE), jnp.float32)
    lower, upper = (0.5, 2.0)
    diagonal = jnp.exp(jax.random.uniform(second_key, (COARSE,), jnp.float32, math.log(lower), math.log(upper)))
    return jnp.diag(diagonal) + 0.15 / math.sqrt(COARSE) * (noise + noise.T)


def shard_levels(key, shape, shards, least, top_value):
    level = 1.0
    for dim, shards_of in shards:
        heights = jax.random.uniform(jax.random.fold_in(jax.random.fold_in(key, 6), dim), (shards_of,), jnp.float32, least / len(shards), top_value / len(shards))
        level = level * jnp.repeat(jnp.exp(heights), shape[dim] // shards_of).reshape((-1,) + (1,) * (len(shape) - 1 - dim))
    return level


def normal_values(rng, dims, spread, bound, shards=(), kind=jnp.bfloat16):
    values = spread * jax.random.normal(rng, dims, jnp.float32)
    if shards:
        values = values * shard_levels(rng, dims, shards, -0.22, 0.18)
    return jnp.clip(values, -bound, bound).astype(kind)


def setup_inputs(seed: int = 0) -> dict:
    streams_of = jax.random.split(jax.random.key(seed), 9)
    schur = draw_schur(jax.random.fold_in(streams_of[8], 71), 0)
    local_gap = normal_values(streams_of[1], (SUBDOMAINS, NB, NRHS), 1.0, 6.0, ((0, 256),), jnp.float32)
    modes = normal_values(streams_of[2], (SUBDOMAINS, MODES, NB), (3.0 / NB ** 0.5), 0.45927933, ((0, 256),), jnp.float32)
    rigid_loads = normal_values(streams_of[3], (SUBDOMAINS, MODES, NRHS), 1.0, 6.0, ((0, 256),), jnp.float32)
    coarse_inverse = draw_coarse_inverse(jax.random.fold_in(streams_of[8], 71), 0)
    block_slot = jax.vmap(lambda own: jax.random.permutation(own, BLOCKS))(jax.random.split(streams_of[5], SUBDOMAINS)).reshape((SUBDOMAINS, BLOCKS)).astype(jnp.int32)
    face_swap = draw_face_swap(jax.random.fold_in(streams_of[8], 71), 0)
    lengths = draw_lengths(jax.random.fold_in(streams_of[8], 71), 0)
    return {"schur": schur, "local_gap": local_gap, "modes": modes, "rigid_loads": rigid_loads, "coarse_inverse": coarse_inverse, "block_slot": block_slot, "face_swap": face_swap, "lengths": lengths}


HIGH = lax.Precision.HIGHEST

def build_layout(block_slot, face_swap, lengths, width):
    blocks = block_slot.shape[1]
    tile = width // blocks
    order = jnp.arange(blocks, dtype=jnp.int32)
    hits = block_slot[:, None, :] == order[None, :, None]
    slot_pos = lax.optimization_barrier(jnp.sum(jnp.where(hits, order[None, None, :], 0), axis=2)).astype(jnp.int32)
    face = (block_slot // 2).astype(jnp.int32)
    copy_index = (block_slot % 2).astype(jnp.int32)
    swapped = jnp.take_along_axis(face_swap, face, axis=1)
    take_index = (face * 2 + (copy_index + swapped) % 2).astype(jnp.int32)
    live = jnp.take_along_axis(lengths, block_slot, axis=1)
    rows = jnp.arange(tile, dtype=jnp.int32)
    mask = (rows[None, None, :, None] < live[:, :, None, None]).astype(jnp.float32)
    return (slot_pos, take_index, mask)

def shift_zero(values, axis, offset):
    extent = values.shape[axis]
    padding = [(0, 0)] * values.ndim
    if offset > 0:
        padding[axis] = (offset, 0)
        return lax.slice_in_dim(jnp.pad(values, padding), 0, extent, axis=axis)
    padding[axis] = (0, -offset)
    return lax.slice_in_dim(jnp.pad(values, padding), -offset, extent - offset, axis=axis)

def exchange_faces(values, layout):
    slot_pos, take_index, mask = layout
    grid = (N_SUB, N_GRP, SUB_DEV, BLOCKS)
    tiles = values.reshape(grid + (BLK, NRHS))
    by_slot = jnp.take_along_axis(tiles, slot_pos.reshape(grid)[..., None, None], axis=3)
    incoming = jnp.concatenate([shift_zero(by_slot[:, :, :, 2:4], 2, 1), shift_zero(by_slot[:, :, :, 0:2], 2, -1), shift_zero(by_slot[:, :, :, 6:8], 1, 1), shift_zero(by_slot[:, :, :, 4:6], 1, -1), jnp.roll(by_slot[:, :, :, 10:12], 1, axis=0), jnp.roll(by_slot[:, :, :, 8:10], -1, axis=0)], axis=3)
    picked = jnp.take_along_axis(incoming, take_index.reshape(grid)[..., None, None], axis=3)
    masks = mask.reshape(grid + (BLK, 1))
    return ((tiles - picked) * masks).reshape(values.shape)

def apply_schur(schur, vector, layout):
    rounded = vector.astype(jnp.bfloat16)

    def single(pair):
        return jnp.dot(pair[0], pair[1], preferred_element_type=jnp.float32)
    return exchange_faces(lax.map(single, (schur, rounded)), layout)

def mode_terms(modes, vector):
    return jnp.einsum('kmn,knr->kmr', modes, vector, precision=HIGH)

def lift(modes, coarse):
    return jnp.einsum('kmn,kmr->knr', modes, coarse, precision=HIGH)

def coarse_solve(coarse_inverse, terms):
    flat = terms.reshape(-1, terms.shape[-1])
    return jnp.dot(coarse_inverse, flat, precision=HIGH).reshape(terms.shape)

def dual_dot(left, right):
    return lax.optimization_barrier(jnp.sum(left * right, axis=(0, 1)))

def reference(schur, local_gap, modes, rigid_loads, coarse_inverse, block_slot, face_swap, lengths):
    layout = build_layout(block_slot, face_swap, lengths, NB)

    def project(vector):
        return vector - exchange_faces(lift(modes, coarse_solve(coarse_inverse, mode_terms(modes, vector))), layout)
    rhs_gap = exchange_faces(local_gap, layout)
    multipliers = exchange_faces(lift(modes, coarse_solve(coarse_inverse, rigid_loads)), layout)
    residual = rhs_gap - apply_schur(schur, multipliers, layout)
    projected = project(residual)
    norm_now = dual_dot(projected, projected)
    first = norm_now
    direction = projected
    for step in range(ITERS):
        image = apply_schur(schur, direction, layout)
        alpha = norm_now / dual_dot(direction, image)
        multipliers = multipliers + alpha * direction
        residual = residual - alpha * image
        projected = project(residual)
        fresh = dual_dot(projected, projected)
        if step + 1 < ITERS:
            direction = projected + fresh / norm_now * direction
        norm_now = fresh
    return (multipliers, jnp.sqrt(norm_now / first))
```

```python
import functools

import jax
import jax.numpy as jnp
from jax import lax
from jax.experimental import pallas as pl
from jax.experimental.pallas import tpu as pltpu
from jax.sharding import Mesh, PartitionSpec as P

BLK = 128
SLOTS = 12
MODES = 6
ROWS = 16
SPLIT_LEFT = (0, 0, 1, 0, 1, 2)
SPLIT_RIGHT = (0, 1, 0, 2, 1, 0)
F32 = jnp.float32
BF16 = jnp.bfloat16
VMEM = pl.BlockSpec(memory_space=pltpu.VMEM)
SMEM = pl.BlockSpec(memory_space=pltpu.SMEM)
ANY = pl.BlockSpec(memory_space=pl.ANY)


def shape(*dims, kind=F32):
    return jax.ShapeDtypeStruct(dims, kind)


def call(kernel, out, in_specs, scratch=(), flops=0, moved=0):
    return pl.pallas_call(
        kernel,
        out_shape=out,
        in_specs=in_specs,
        out_specs=jax.tree.map(lambda _: VMEM, out),
        scratch_shapes=list(scratch),
        compiler_params=pltpu.CompilerParams(vmem_limit_bytes=50 * 2**20),
        cost_estimate=pl.CostEstimate(flops=flops, bytes_accessed=moved, transcendentals=0),
    )


def thirds(value):
    first = value.astype(BF16)
    rest = value - first.astype(F32)
    second = rest.astype(BF16)
    third = (rest - second.astype(F32)).astype(BF16)
    return first, second, third


def modes_kernel(slot_ref, modes_ref, split_ref, *rest):
    parts, by_slot = rest[:5], rest[5]
    by_slot[...] = jnp.zeros_like(by_slot)
    for k in range(2):
        for b in range(SLOTS):
            by_slot[k, slot_ref[k, b], 0:MODES] = modes_ref[k, :, b * BLK:(b + 1) * BLK]
    parts[0][...] = by_slot[:, 0:4]
    for n in range(4):
        parts[n + 1][...] = by_slot[:, 4 + 2 * n:6 + 2 * n]
    for k in range(2):
        for q in range(SLOTS):
            pieces = [piece.astype(F32) for piece in thirds(by_slot[k, q])]
            pieces.append(jnp.zeros_like(pieces[0]))
            split_ref[k, :, q * BLK:(q + 1) * BLK] = jnp.concatenate(pieces, axis=0).astype(BF16)


def arrange_modes(slots, modes):
    return call(
        modes_kernel,
        (shape(2, 32, SLOTS * BLK, kind=BF16), shape(2, 4, 8, BLK)) + (shape(2, 2, 8, BLK),) * 4,
        [SMEM, VMEM],
        [pltpu.VMEM((2, SLOTS, 8, BLK), F32)],
    )(slots, modes)


def partner(parts, arrived, swap_ref, k, f, c):
    meets = jnp.bitwise_xor(swap_ref[k, f], c)
    if f == 0:
        return parts[0][1 - k, 2 + meets]
    if f == 1:
        return parts[0][1 - k, meets]
    return arrived[f - 2][k, meets]


def own(parts, k, f, c):
    return parts[0][k, 2 * f + c] if f < 2 else parts[f - 1][k, c]


def partial_kernel(before_ref, here_ref, after_ref, terms_ref, out_ref):
    terms = terms_ref[...].reshape(-1, BLK)
    high = functools.partial(jnp.dot, precision=lax.Precision.HIGHEST, preferred_element_type=F32)
    before = high(before_ref[...], terms)
    here = high(here_ref[...], terms)
    after = high(after_ref[...], terms)
    tables = [before, here[0:64], here[64:128], after]
    sums = jnp.sum(terms_ref[:, 8:16, :], axis=0)
    upper = lax.broadcasted_iota(jnp.int32, (8, BLK), 0) >= 4

    def rows(table, x):
        return tables[table][x * ROWS:(x + 1) * ROWS]

    for core in range(2):
        for x in range(4):
            d = core * 4 + x
            mine = rows(1 + core, x)
            out_ref[d, 0, 0:8] = mine[0:8]
            out_ref[d, 0, 8:16] = jnp.where(upper, sums, mine[8:16])
            out_ref[d, 1] = rows(1 + core, max(x - 1, 0))
            out_ref[d, 2] = rows(1 + core, min(x + 1, 3))
            out_ref[d, 3] = rows(core, x)
            out_ref[d, 4] = rows(2 + core, x)


def coarse_solve(table, terms):
    gathered = lax.all_to_all(terms, "p", 0, 0, tiled=True)
    partial = call(partial_kernel, shape(8, 5, ROWS, BLK), [VMEM] * 4)(*table, gathered)
    return lax.all_to_all(partial, ("core", "x"), 0, 0, tiled=True)


def load_coefficients(partial_ref, coef_ref):
    solved = jnp.sum(partial_ref[...], axis=0)
    coef_ref[...] = jnp.zeros_like(coef_ref)
    for k in range(2):
        lines = slice(MODES * k, MODES * (k + 1))
        other = slice(MODES * (1 - k), MODES * (2 - k))
        for f in range(6):
            coef_ref[k, f, 0:MODES] = solved[0, lines]
            coef_ref[k, f, MODES:2 * MODES] = solved[0, other] if f < 2 else solved[f - 1, lines]
    return solved[0]


def lifted(lift_ref, coef_ref, k, f):
    pieces = thirds(coef_ref[k, f])
    right = jnp.concatenate([pieces[n] for n in SPLIT_RIGHT], axis=0)
    return jnp.dot(lift_ref[k, f], right, preferred_element_type=F32)


def fetch_schur(schur_ref, held, sems):
    copies = []
    for k in range(2):
        for n in range(3):
            rows = pl.ds(n * 512, 512)
            copy = pltpu.make_async_copy(schur_ref.at[k, rows], held.at[k, rows], sems.at[3 * k + n])
            copy.start()
            copies.append(copy)
    return copies


def apply_schur(copies, held, rounded, slot_ref, by_slot, parts, base=None):
    for k in range(2):
        for n in range(3):
            copies[3 * k + n].wait()
            image = jnp.dot(held[k, n * 512:(n + 1) * 512], rounded[k], preferred_element_type=F32)
            for j in range(4):
                b = 4 * n + j
                piece = image[j * BLK:(j + 1) * BLK]
                if base is not None:
                    piece = base[k, b * BLK:(b + 1) * BLK] - piece
                by_slot[slot_ref[k, b]] = piece
        parts[0][k] = by_slot[0:4]
        for n in range(4):
            parts[n + 1][k] = by_slot[4 + 2 * n:6 + 2 * n]


def round_blocks(field_ref, slot_ref, rounded):
    for k in range(2):
        for b in range(SLOTS):
            rounded[k, b * BLK:(b + 1) * BLK] = field_ref[k, slot_ref[k, b]].astype(BF16)


PARTS = (shape(2, 4, BLK, BLK),) + (shape(2, 2, BLK, BLK),) * 4
FIELD = shape(2, SLOTS, BLK, BLK)
SCRATCH = [
    pltpu.VMEM((2, 6, ROWS, BLK), F32),
    pltpu.VMEM((2, SLOTS * BLK, SLOTS * BLK), BF16),
    pltpu.VMEM((2, SLOTS * BLK, BLK), BF16),
    pltpu.VMEM((SLOTS, BLK, BLK), F32),
    pltpu.SemaphoreType.DMA((6,)),
]


def first_kernel(slot_ref, swap_ref, length_ref, partial_ref, gap_ref, schur_ref, *rest):
    parts, arrived = rest[0:5], rest[5:9]
    lift_ref, field_ref = rest[9:11]
    images = rest[11:16]
    coef_ref, held, rounded, by_slot, sems = rest[16:]
    copies = fetch_schur(schur_ref, held, sems)
    lane = lax.broadcasted_iota(jnp.int32, (8, BLK), 1)
    for k in range(2):
        for f in range(6):
            for c in range(2):
                live = lane < length_ref[k, 2 * f + c]
                mine = jnp.where(live, own(parts, k, f, c), 0.0)
                theirs = jnp.where(live, -partner(parts, arrived, swap_ref, k, f, c), 0.0)
                both = jnp.concatenate([mine[0:MODES], theirs[0:MODES], mine[MODES:8], mine[MODES:8]], axis=0)
                pieces = [piece.astype(F32) for piece in thirds(both)]
                left = jnp.concatenate([pieces[n] for n in SPLIT_LEFT], axis=0)
                lift_ref[k, f, c * BLK:(c + 1) * BLK] = left.T.astype(BF16)
    load_coefficients(partial_ref, coef_ref)
    for k in range(2):
        for f in range(6):
            field_ref[k, 2 * f:2 * f + 2] = lifted(lift_ref, coef_ref, k, f).reshape(2, BLK, BLK)
    round_blocks(field_ref, slot_ref, rounded)
    apply_schur(copies, held, rounded, slot_ref, by_slot, images, gap_ref)


def project_kernel(slot_ref, partial_ref, lift_ref, schur_ref, residual_ref, *rest):
    field_ref, images = rest[0], rest[1:6]
    coef_ref, held, rounded, by_slot, sems = rest[6:]
    copies = fetch_schur(schur_ref, held, sems)
    load_coefficients(partial_ref, coef_ref)
    for k in range(2):
        for f in range(6):
            lift = lifted(lift_ref, coef_ref, k, f).reshape(2, BLK, BLK)
            field_ref[k, 2 * f:2 * f + 2] = residual_ref[k, 2 * f:2 * f + 2] - lift
    round_blocks(field_ref, slot_ref, rounded)
    apply_schur(copies, held, rounded, slot_ref, by_slot, images)


def step_kernel(slot_ref, partial_ref, lift_ref, schur_ref, image_ref, projected_ref, *rest):
    sums_ref, change_ref, field_ref, images = rest[0], rest[1], rest[2], rest[3:8]
    coef_ref, held, rounded, by_slot, sems = rest[8:]
    copies = fetch_schur(schur_ref, held, sems)
    sums = load_coefficients(partial_ref, coef_ref)[8:16]
    sums_ref[...] = sums
    alpha = sums[4:5] / sums[5:6]
    for k in range(2):
        for f in range(6):
            pair = slice(2 * f, 2 * f + 2)
            change = image_ref[k, pair] - lifted(lift_ref, coef_ref, k, f).reshape(2, BLK, BLK)
            change_ref[k, pair] = change
            field_ref[k, pair] = projected_ref[k, pair] - alpha[None] * change
    round_blocks(field_ref, slot_ref, rounded)
    apply_schur(copies, held, rounded, slot_ref, by_slot, images)


def last_kernel(
    slot_ref, partial_ref, lift_ref, sums_ref, start_ref, first_ref, change_ref, second_ref, image_ref,
    multipliers_ref, norm_ref, coef_ref, by_slot,
):
    riders = load_coefficients(partial_ref, coef_ref)
    start_norm, start_curve = sums_ref[4:5], sums_ref[5:6]
    norm, second_curve, cross, back = riders[12:13], riders[13:14], riders[14:15], riders[15:16]
    alpha = start_norm / start_curve
    beta = norm / start_norm
    curve = second_curve + beta * (cross + back) + beta * beta * start_curve
    step = norm / curve
    total = jnp.zeros((1, BLK), F32)
    for k in range(2):
        for f in range(6):
            pair = slice(2 * f, 2 * f + 2)
            lift = lifted(lift_ref, coef_ref, k, f).reshape(2, BLK, BLK)
            change = (image_ref[k, pair] - lift) + beta[None] * change_ref[k, pair]
            second = second_ref[k, pair]
            left = second - step[None] * change
            total = total + jnp.sum((left * left).reshape(2 * BLK, BLK), axis=0, keepdims=True)
            first = first_ref[k, pair]
            direction = second + beta[None] * first
            by_slot[pair] = (start_ref[k, pair] + alpha[None] * first) + step[None] * direction
        for b in range(SLOTS):
            multipliers_ref[k, b * BLK:(b + 1) * BLK] = by_slot[slot_ref[k, b]]
    norm_ref[...] = jnp.broadcast_to(total[None], norm_ref.shape)


def combine_kernel(dots, swap_ref, length_ref, split_ref, *rest):
    parts, arrived = rest[0:5], rest[5:9]
    extras, (field_ref, terms_ref, line_ref) = rest[9:-3], rest[-3:]
    row = lax.broadcasted_iota(jnp.int32, (BLK, BLK), 0)
    line_ref[...] = jnp.zeros_like(line_ref)
    totals = [jnp.zeros((8, BLK), F32) for _ in dots]
    for k in range(2):
        for f in range(6):
            for c in range(2):
                q = 2 * f + c
                gap = own(parts, k, f, c) - partner(parts, arrived, swap_ref, k, f, c)
                block = jnp.where(row < length_ref[k, q], gap, 0.0)
                field_ref[k, q] = block
                for n, (left, right) in enumerate(dots):
                    a = block if left is None else extras[left][k, q]
                    b = block if right is None else extras[right][k, q]
                    totals[n] = totals[n] + jnp.sum((a * b).reshape(BLK // 8, 8, BLK), axis=0)
        pieces = thirds(field_ref[k].reshape(SLOTS * BLK, BLK))
        one = jnp.dot(split_ref[k], pieces[0], preferred_element_type=F32)
        two = jnp.dot(split_ref[k], pieces[1], preferred_element_type=F32)
        three = jnp.dot(split_ref[k], pieces[2], preferred_element_type=F32)
        terms = one[0:8] + ((one[8:16] + two[0:8]) + ((one[16:24] + two[8:16]) + three[0:8]))
        line_ref[MODES * k:MODES * (k + 1)] = terms[0:MODES]
    for n, total in enumerate(totals):
        line_ref[12 + n:13 + n] = jnp.sum(total, axis=0, keepdims=True)
    terms_ref[...] = jnp.broadcast_to(line_ref[...][None], terms_ref.shape)


def send(parts):
    def moved(value, axis, step):
        count = lax.axis_size(axis)
        return lax.ppermute(value, axis, [(i, (i + step) % count) for i in range(count)])

    sub = ("p", "core")
    return (
        moved(parts[2], "x", 1), moved(parts[1], "x", -1),
        moved(parts[4], sub, 1), moved(parts[3], sub, -1),
    )


def combine(dots, places, swaps, lengths, split, parts, *extras):
    kernel = functools.partial(combine_kernel, dots)
    out = (FIELD, shape(places, ROWS, BLK))
    specs = [SMEM] * 2 + [VMEM] * (10 + len(extras))
    return call(kernel, out, specs, [pltpu.VMEM((ROWS, BLK), F32)])(
        swaps, lengths, split, *parts, *send(parts), *extras
    )


def coarse_table(coarse_inverse, places):
    group = min(places, 8)
    span = group * 8 * MODES * 2
    line = jnp.arange(span, dtype=jnp.int32)[:, None]
    lane = jnp.arange(8 * group * ROWS, dtype=jnp.int32)[None, :]
    inner, spot, kind = lane % ROWS, (lane // ROWS) % group, lane // (ROWS * group)
    pick = jnp.where((line == spot * 96 + kind * 12 + inner) & (inner < 12), 1.0, 0.0).astype(F32)
    sorted_columns = jnp.einsum(
        "rgj,jl->rgl", coarse_inverse.reshape(12, places // group, span), pick, precision=lax.Precision.HIGHEST
    )
    by_kind = sorted_columns.reshape(12, places // group, 8, group * ROWS).transpose(2, 0, 1, 3)
    by_kind = jnp.pad(by_kind.reshape(8, 12, places * ROWS), ((0, 0), (0, 4), (0, 0)))
    here = lax.all_to_all(by_kind, ("core", "x"), 0, 0, tiled=True)
    before = lax.ppermute(here[4:8], "p", [(i, (i + 1) % places) for i in range(places)])
    after = lax.ppermute(here[0:4], "p", [(i, (i - 1) % places) for i in range(places)])
    return tuple(part.reshape(-1, places * ROWS) for part in (before, here, after))


def body(schur, local_gap, modes, rigid_loads, coarse_inverse, slots, swaps, lengths):
    places = lax.axis_size("p")
    loads = jnp.pad(rigid_loads.reshape(2 * MODES, BLK), ((0, 4), (0, 0)))
    loads = jnp.broadcast_to(loads[None], (places, ROWS, BLK))
    table = coarse_table(coarse_inverse, places)
    split, *mode_parts = arrange_modes(slots, modes)
    mode_arrived = send(mode_parts)
    operator_flops = 2 * 2 * SLOTS * BLK * SLOTS * BLK * BLK
    operator_bytes = 2 * SLOTS * BLK * SLOTS * BLK * 2

    partial = coarse_solve(table, loads)
    lift, start, *images = call(
        first_kernel,
        (shape(2, 6, 2 * BLK, 6 * ROWS, kind=BF16), FIELD) + PARTS,
        [SMEM] * 3 + [VMEM] * 2 + [ANY] + [VMEM] * 9,
        SCRATCH, operator_flops, operator_bytes,
    )(slots, swaps, lengths, partial, local_gap, schur, *mode_parts, *mode_arrived)
    residual, terms = combine((), places, swaps, lengths, split, images)

    partial = coarse_solve(table, terms)
    projected, *images = call(
        project_kernel, (FIELD,) + PARTS, [SMEM] + [VMEM] * 2 + [ANY, VMEM], SCRATCH, operator_flops, operator_bytes
    )(slots, partial, lift, schur, residual)
    image, terms = combine(((0, 0), (0, None)), places, swaps, lengths, split, images, projected)

    partial = coarse_solve(table, terms)
    sums, change, second, *images = call(
        step_kernel, (shape(8, BLK), FIELD, FIELD) + PARTS, [SMEM] + [VMEM] * 2 + [ANY] + [VMEM] * 2,
        SCRATCH, operator_flops, operator_bytes,
    )(slots, partial, lift, schur, image, projected)
    dots = ((0, 0), (0, None), (1, None), (0, 2))
    second_image, terms = combine(dots, places, swaps, lengths, split, images, second, projected, image)

    partial = coarse_solve(table, terms)
    multipliers, norm = call(
        last_kernel, (shape(2, SLOTS * BLK, BLK), shape(places, 8, BLK)), [SMEM] + [VMEM] * 8,
        [SCRATCH[0], SCRATCH[3]],
    )(slots, partial, lift, sums, start, projected, change, second, second_image)
    norm = jnp.sum(lax.all_to_all(norm, "p", 0, 0, tiled=True), axis=0)
    norm = lax.all_to_all(jnp.broadcast_to(norm[None], (8, 8, BLK)), ("core", "x"), 0, 0, tiled=True)
    return multipliers, jnp.sqrt(jnp.sum(norm[:, 0], axis=0) / sums[4])


def solution(mesh):
    fine = Mesh(mesh.devices.reshape(-1, 2, 4), ("p", "core", "x"))
    everywhere = ("p", "core", "x")
    deep, flat = P(everywhere, None, None), P(everywhere, None)
    in_specs = (deep, deep, deep, deep, flat, flat, flat, flat)
    return jax.shard_map(body, mesh=fine, in_specs=in_specs, out_specs=(deep, P()), check_vma=False)
```

```python
import functools

import jax
import jax.numpy as jnp
from jax import lax
from jax.experimental import pallas as pl
from jax.experimental.pallas import tpu as pltpu
from jax.sharding import Mesh, PartitionSpec as P

BLK = 128
SLOTS = 12
MODES = 6
ROWS = 16
SPLIT_LEFT = (0, 0, 1, 0, 1, 2)
SPLIT_RIGHT = (0, 1, 0, 2, 1, 0)
F32 = jnp.float32
BF16 = jnp.bfloat16
VMEM = pl.BlockSpec(memory_space=pltpu.VMEM)
SMEM = pl.BlockSpec(memory_space=pltpu.SMEM)


def shape(*dims, kind=F32):
    return jax.ShapeDtypeStruct(dims, kind)


def call(kernel, out, in_specs, scratch=(), flops=0, moved=0):
    return pl.pallas_call(
        kernel,
        out_shape=out,
        in_specs=in_specs,
        out_specs=jax.tree.map(lambda _: VMEM, out),
        scratch_shapes=list(scratch),
        compiler_params=pltpu.CompilerParams(vmem_limit_bytes=24 * 2**20),
        cost_estimate=pl.CostEstimate(flops=flops, bytes_accessed=moved, transcendentals=0),
    )


def thirds(value):
    first = value.astype(BF16)
    rest = value - first.astype(F32)
    second = rest.astype(BF16)
    third = (rest - second.astype(F32)).astype(BF16)
    return first, second, third


def pack_kernel(slot_ref, modes_ref, loads_ref, coarse_ref, split_ref, payload_ref, *rest):
    parts, (by_slot, rows, line) = rest[:5], rest[5:]
    by_slot[...] = jnp.zeros_like(by_slot)
    for k in range(2):
        for b in range(SLOTS):
            for i in range(MODES):
                by_slot[k, slot_ref[k, b], i:i + 1] = modes_ref[i, k:k + 1, b * BLK:(b + 1) * BLK]
    parts[0][...] = by_slot[:, 0:4]
    for n in range(4):
        parts[n + 1][...] = by_slot[:, 4 + 2 * n:6 + 2 * n]
    rows[...] = jnp.zeros_like(rows)
    rows[0:12] = coarse_ref[...]
    line[...] = jnp.zeros_like(line)
    for k in range(2):
        for i in range(MODES):
            line[k * MODES + i:k * MODES + i + 1] = loads_ref[i, k:k + 1]
    places, tiles = payload_ref.shape[0], rows.shape[1] // BLK
    left = lax.broadcasted_iota(jnp.int32, (MODES, BLK), 1) < 64
    for p in range(places):
        first = (96 * p - 48) % (96 * places)
        tile, shift = first // BLK, first % BLK
        wide = [rows[:, (tile + j) % tiles * BLK:((tile + j) % tiles + 1) * BLK] for j in range(3)]
        window = pltpu.roll(jnp.concatenate(wide, axis=1), 3 * BLK - shift, axis=1)
        tail = window[:, BLK:2 * BLK]
        payload_ref[p, 0:12] = window[0:12, 0:BLK]
        payload_ref[p, 12:18] = jnp.where(left, tail[0:6], pltpu.roll(tail, 64, axis=1)[6:12])
        payload_ref[p, 18:32] = line[0:14]
    for k in range(2):
        for q in range(SLOTS):
            pieces = [piece.astype(F32) for piece in thirds(by_slot[k, q])]
            pieces.append(jnp.zeros_like(pieces[0]))
            split_ref[k, :, q * BLK:(q + 1) * BLK] = jnp.concatenate(pieces, axis=0).astype(BF16)


def pack(slots, modes, loads, coarse_inverse, places):
    return call(
        pack_kernel,
        (shape(2, 32, SLOTS * BLK, kind=BF16), shape(places, 32, BLK), shape(2, 4, 8, BLK))
        + (shape(2, 2, 8, BLK),) * 4,
        [SMEM] + [VMEM] * 3,
        [pltpu.VMEM((2, SLOTS, 8, BLK), F32), pltpu.VMEM((ROWS, 96 * places), F32), pltpu.VMEM((ROWS, BLK), F32)],
    )(slots, modes.transpose(1, 0, 2), loads.transpose(1, 0, 2), coarse_inverse)


def partner(parts, arrived, swap_ref, k, f, c):
    meets = jnp.bitwise_xor(swap_ref[k, f], c)
    if f == 0:
        return parts[0][1 - k, 2 + meets]
    if f == 1:
        return parts[0][1 - k, meets]
    return arrived[f - 2][k, meets]


def own(parts, k, f, c):
    return parts[0][k, 2 * f + c] if f < 2 else parts[f - 1][k, c]


def share(core, table, terms, riders, mine_ref, other_ref, solved):
    result = jnp.dot(table, terms, precision=lax.Precision.HIGHEST, preferred_element_type=F32)
    for n in range(4):
        for x in range(4):
            solved[n, x, 0:12] = result[(4 * n + x) * 12:(4 * n + x + 1) * 12]
    for out_ref, c in ((mine_ref, core), (other_ref, 1 - core)):
        for x in range(4):
            out_ref[x, 0:12] = solved[c + 1, x, 0:12]
            out_ref[x, 12:16] = riders
            out_ref[x, 16:28] = solved[c + 1, max(x - 1, 0), 0:12]
            out_ref[x, 28:40] = solved[c + 1, min(x + 1, 3), 0:12]
            out_ref[x, 40:52] = solved[c, x, 0:12]
            out_ref[x, 52:64] = solved[c + 2, x, 0:12]


def partial_kernel(core_ref, table_ref, terms_ref, mine_ref, other_ref, solved):
    riders = jnp.sum(terms_ref[:, 8:16], axis=0)[4:8]
    share(core_ref[0], table_ref[...], terms_ref[...].reshape(-1, BLK), riders, mine_ref, other_ref, solved)


def unpack_kernel(core_ref, swap_ref, length_ref, payload_ref, *rest):
    parts, arrived = rest[0:5], rest[5:9]
    table_ref, lift_ref, mine_ref, other_ref, wide, terms, solved = rest[9:]
    places = payload_ref.shape[0]
    terms[...] = jnp.zeros_like(terms)
    wide[...] = jnp.zeros_like(wide)
    for p in range(places):
        tail = payload_ref[p, 12:18]
        wide[ROWS * p:ROWS * p + 12, 0:BLK] = payload_ref[p, 0:12]
        wide[ROWS * p:ROWS * p + 6, BLK:2 * BLK] = tail
        wide[ROWS * p + 6:ROWS * p + 12, BLK:2 * BLK] = pltpu.roll(tail, 64, axis=1)
        terms[ROWS * p:ROWS * p + 12] = payload_ref[p, 18:30]
    table_ref[...] = wide[...].T[0:192]
    riders = jnp.zeros((4, BLK), F32)
    share(core_ref[0], table_ref[...], terms[...], riders, mine_ref, other_ref, solved)
    lane = lax.broadcasted_iota(jnp.int32, (8, BLK), 1)
    for k in range(2):
        for f in range(6):
            for c in range(2):
                live = lane < length_ref[k, 2 * f + c]
                mine = jnp.where(live, own(parts, k, f, c), 0.0)
                theirs = jnp.where(live, -partner(parts, arrived, swap_ref, k, f, c), 0.0)
                both = jnp.concatenate([mine[0:MODES], theirs[0:MODES], mine[MODES:8], mine[MODES:8]], axis=0)
                pieces = [piece.astype(F32) for piece in thirds(both)]
                left = jnp.concatenate([pieces[n] for n in SPLIT_LEFT], axis=0)
                lift_ref[k, f, c * BLK:(c + 1) * BLK] = left.T.astype(BF16)


SHARES = (shape(4, 64, BLK), shape(4, 64, BLK))
SOLVED = pltpu.VMEM((4, 4, ROWS, BLK), F32)


def unpack(core, swaps, lengths, payload, parts):
    places = payload.shape[0]
    payload = lax.all_to_all(payload, "p", 0, 0, tiled=True)
    return call(
        unpack_kernel,
        (shape(192, places * ROWS), shape(2, 6, 2 * BLK, 6 * ROWS, kind=BF16)) + SHARES,
        [SMEM] * 3 + [VMEM] * 10,
        [pltpu.VMEM((places * ROWS, 2 * BLK), F32), pltpu.VMEM((places * ROWS, BLK), F32), SOLVED],
    )(core, swaps, lengths, payload, *parts, *send(parts))


def collect(mine, other):
    both = mine + lax.ppermute(other, "core", [(0, 1), (1, 0)])
    return lax.all_to_all(both, "x", 0, 0, tiled=True)


def coarse_solve(core, table, terms):
    gathered = lax.all_to_all(terms, "p", 0, 0, tiled=True)
    return collect(*call(partial_kernel, SHARES, [SMEM] + [VMEM] * 2, [SOLVED])(core, table, gathered))


def load_coefficients(partial_ref, coef_ref):
    solved = jnp.sum(partial_ref[...], axis=0)
    coef_ref[...] = jnp.zeros_like(coef_ref)
    for k in range(2):
        other = MODES * (1 - k)
        firsts = [other, other] + [16 + 12 * n + MODES * k for n in range(4)]
        for f in range(6):
            coef_ref[k, f, 0:MODES] = solved[MODES * k:MODES * (k + 1)]
            coef_ref[k, f, MODES:2 * MODES] = solved[firsts[f]:firsts[f] + MODES]
    return solved[0:16]


def lifted(lift_ref, coef_ref, k, f):
    pieces = thirds(coef_ref[k, f])
    right = jnp.concatenate([pieces[n] for n in SPLIT_RIGHT], axis=0)
    return jnp.dot(lift_ref[k, f], right, preferred_element_type=F32)


def apply_schur(schur_ref, rounded, slot_ref, by_slot, parts, base=None):
    for k in range(2):
        for n in range(3):
            image = jnp.dot(schur_ref[k, n * 512:(n + 1) * 512], rounded[k], preferred_element_type=F32)
            for j in range(4):
                b = 4 * n + j
                piece = image[j * BLK:(j + 1) * BLK]
                if base is not None:
                    piece = base[k, b * BLK:(b + 1) * BLK] - piece
                by_slot[slot_ref[k, b]] = piece
        parts[0][k] = by_slot[0:4]
        for n in range(4):
            parts[n + 1][k] = by_slot[4 + 2 * n:6 + 2 * n]


def round_blocks(field_ref, slot_ref, rounded):
    for k in range(2):
        for b in range(SLOTS):
            rounded[k, b * BLK:(b + 1) * BLK] = field_ref[k, slot_ref[k, b]].astype(BF16)


PARTS = (shape(2, 4, BLK, BLK),) + (shape(2, 2, BLK, BLK),) * 4
FIELD = shape(2, SLOTS, BLK, BLK)
SCRATCH = [
    pltpu.VMEM((2, 6, ROWS, BLK), F32),
    pltpu.VMEM((2, SLOTS * BLK, BLK), BF16),
    pltpu.VMEM((SLOTS, BLK, BLK), F32),
]


def first_kernel(slot_ref, partial_ref, lift_ref, schur_ref, gap_ref, *rest):
    field_ref, images = rest[0], rest[1:6]
    coef_ref, rounded, by_slot = rest[6:]
    load_coefficients(partial_ref, coef_ref)
    for k in range(2):
        for f in range(6):
            field_ref[k, 2 * f:2 * f + 2] = lifted(lift_ref, coef_ref, k, f).reshape(2, BLK, BLK)
    round_blocks(field_ref, slot_ref, rounded)
    apply_schur(schur_ref, rounded, slot_ref, by_slot, images, gap_ref)


def project_kernel(slot_ref, partial_ref, lift_ref, schur_ref, residual_ref, *rest):
    field_ref, images = rest[0], rest[1:6]
    coef_ref, rounded, by_slot = rest[6:]
    load_coefficients(partial_ref, coef_ref)
    for k in range(2):
        for f in range(6):
            lift = lifted(lift_ref, coef_ref, k, f).reshape(2, BLK, BLK)
            field_ref[k, 2 * f:2 * f + 2] = residual_ref[k, 2 * f:2 * f + 2] - lift
    round_blocks(field_ref, slot_ref, rounded)
    apply_schur(schur_ref, rounded, slot_ref, by_slot, images)


def step_kernel(slot_ref, partial_ref, lift_ref, schur_ref, image_ref, projected_ref, *rest):
    sums_ref, change_ref, field_ref, images = rest[0], rest[1], rest[2], rest[3:8]
    coef_ref, rounded, by_slot = rest[8:]
    sums = load_coefficients(partial_ref, coef_ref)[8:16]
    sums_ref[...] = sums
    alpha = sums[4:5] / sums[5:6]
    for k in range(2):
        for f in range(6):
            pair = slice(2 * f, 2 * f + 2)
            change = image_ref[k, pair] - lifted(lift_ref, coef_ref, k, f).reshape(2, BLK, BLK)
            change_ref[k, pair] = change
            field_ref[k, pair] = projected_ref[k, pair] - alpha[None] * change
    round_blocks(field_ref, slot_ref, rounded)
    apply_schur(schur_ref, rounded, slot_ref, by_slot, images)


def last_kernel(
    slot_ref, partial_ref, lift_ref, sums_ref, start_ref, first_ref, change_ref, second_ref, image_ref,
    multipliers_ref, norm_ref, coef_ref, by_slot,
):
    riders = load_coefficients(partial_ref, coef_ref)
    start_norm, start_curve = sums_ref[4:5], sums_ref[5:6]
    norm, second_curve, cross, back = riders[12:13], riders[13:14], riders[14:15], riders[15:16]
    alpha = start_norm / start_curve
    beta = norm / start_norm
    curve = second_curve + beta * (cross + back) + beta * beta * start_curve
    step = norm / curve
    total = jnp.zeros((1, BLK), F32)
    for k in range(2):
        for f in range(6):
            pair = slice(2 * f, 2 * f + 2)
            lift = lifted(lift_ref, coef_ref, k, f).reshape(2, BLK, BLK)
            change = (image_ref[k, pair] - lift) + beta[None] * change_ref[k, pair]
            second = second_ref[k, pair]
            left = second - step[None] * change
            total = total + jnp.sum((left * left).reshape(2 * BLK, BLK), axis=0, keepdims=True)
            first = first_ref[k, pair]
            direction = second + beta[None] * first
            by_slot[pair] = (start_ref[k, pair] + alpha[None] * first) + step[None] * direction
        for b in range(SLOTS):
            multipliers_ref[k, b * BLK:(b + 1) * BLK] = by_slot[slot_ref[k, b]]
    norm_ref[...] = jnp.broadcast_to(total[None], norm_ref.shape)


def combine_kernel(dots, swap_ref, length_ref, split_ref, *rest):
    parts, arrived = rest[0:5], rest[5:9]
    extras, (field_ref, terms_ref, line_ref) = rest[9:-3], rest[-3:]
    row = lax.broadcasted_iota(jnp.int32, (BLK, BLK), 0)
    line_ref[...] = jnp.zeros_like(line_ref)
    totals = [jnp.zeros((8, BLK), F32) for _ in dots]
    for k in range(2):
        for f in range(6):
            for c in range(2):
                q = 2 * f + c
                gap = own(parts, k, f, c) - partner(parts, arrived, swap_ref, k, f, c)
                block = jnp.where(row < length_ref[k, q], gap, 0.0)
                field_ref[k, q] = block
                for n, (left, right) in enumerate(dots):
                    a = block if left is None else extras[left][k, q]
                    b = block if right is None else extras[right][k, q]
                    totals[n] = totals[n] + jnp.sum((a * b).reshape(BLK // 8, 8, BLK), axis=0)
        pieces = thirds(field_ref[k].reshape(SLOTS * BLK, BLK))
        one = jnp.dot(split_ref[k], pieces[0], preferred_element_type=F32)
        two = jnp.dot(split_ref[k], pieces[1], preferred_element_type=F32)
        three = jnp.dot(split_ref[k], pieces[2], preferred_element_type=F32)
        terms = one[0:8] + ((one[8:16] + two[0:8]) + ((one[16:24] + two[8:16]) + three[0:8]))
        line_ref[MODES * k:MODES * (k + 1)] = terms[0:MODES]
    for n, total in enumerate(totals):
        line_ref[12 + n:13 + n] = jnp.sum(total, axis=0, keepdims=True)
    terms_ref[...] = jnp.broadcast_to(line_ref[...][None], terms_ref.shape)


def send(parts):
    def moved(value, axis, step):
        count = lax.axis_size(axis)
        return lax.ppermute(value, axis, [(i, (i + step) % count) for i in range(count)])

    sub = ("p", "core")
    return (
        moved(parts[2], "x", 1), moved(parts[1], "x", -1),
        moved(parts[4], sub, 1), moved(parts[3], sub, -1),
    )


def combine(dots, places, swaps, lengths, split, parts, *extras):
    kernel = functools.partial(combine_kernel, dots)
    out = (FIELD, shape(places, ROWS, BLK))
    specs = [SMEM] * 2 + [VMEM] * (10 + len(extras))
    return call(kernel, out, specs, [pltpu.VMEM((ROWS, BLK), F32)])(
        swaps, lengths, split, *parts, *send(parts), *extras
    )


def body(schur, local_gap, modes, rigid_loads, coarse_inverse, slots, swaps, lengths):
    places = lax.axis_size("p")
    core = jnp.full((1,), lax.axis_index("core"), jnp.int32)
    operator_flops = 2 * 2 * SLOTS * BLK * SLOTS * BLK * BLK
    operator_bytes = 2 * SLOTS * BLK * SLOTS * BLK * 2

    split, payload, *mode_parts = pack(slots, modes, rigid_loads, coarse_inverse, places)
    table, lift, *shares = unpack(core, swaps, lengths, payload, mode_parts)
    partial = collect(*shares)
    start, *images = call(
        first_kernel, (FIELD,) + PARTS, [SMEM] + [VMEM] * 4, SCRATCH, operator_flops, operator_bytes
    )(slots, partial, lift, schur, local_gap)
    residual, terms = combine((), places, swaps, lengths, split, images)

    partial = coarse_solve(core, table, terms)
    projected, *images = call(
        project_kernel, (FIELD,) + PARTS, [SMEM] + [VMEM] * 4, SCRATCH, operator_flops, operator_bytes
    )(slots, partial, lift, schur, residual)
    image, terms = combine(((0, 0), (0, None)), places, swaps, lengths, split, images, projected)

    partial = coarse_solve(core, table, terms)
    sums, change, second, *images = call(
        step_kernel, (shape(8, BLK), FIELD, FIELD) + PARTS, [SMEM] + [VMEM] * 5,
        SCRATCH, operator_flops, operator_bytes,
    )(slots, partial, lift, schur, image, projected)
    dots = ((0, 0), (0, None), (1, None), (0, 2))
    second_image, terms = combine(dots, places, swaps, lengths, split, images, second, projected, image)

    partial = coarse_solve(core, table, terms)
    multipliers, norm = call(
        last_kernel, (shape(2, SLOTS * BLK, BLK), shape(places, 8, BLK)), [SMEM] + [VMEM] * 8,
        [SCRATCH[0], SCRATCH[2]],
    )(slots, partial, lift, sums, start, projected, change, second, second_image)
    norm = jnp.sum(lax.all_to_all(norm, "p", 0, 0, tiled=True), axis=0)
    norm = norm + lax.ppermute(norm, "core", [(0, 1), (1, 0)])
    norm = lax.all_to_all(jnp.broadcast_to(norm[None], (4, 8, BLK)), "x", 0, 0, tiled=True)
    return multipliers, jnp.sqrt(jnp.sum(norm[:, 0], axis=0) / sums[4])


def solution(mesh):
    fine = Mesh(mesh.devices.reshape(-1, 2, 4), ("p", "core", "x"))
    everywhere = ("p", "core", "x")
    deep, flat = P(everywhere, None, None), P(everywhere, None)
    in_specs = (deep, deep, deep, deep, flat, flat, flat, flat)
    return jax.shard_map(body, mesh=fine, in_specs=in_specs, out_specs=(deep, P()), check_vma=False)
```

```python
import functools

import jax
import jax.numpy as jnp
from jax import lax
from jax.experimental import pallas as pl
from jax.experimental.pallas import tpu as pltpu
from jax.sharding import Mesh, PartitionSpec as P

BLK = 128
SLOTS = 12
MODES = 6
ROWS = 16
PACK_ROOM = 60
NORM_ROWS = 1
SPLIT_LEFT = (0, 0, 1, 0, 1, 2)
SPLIT_RIGHT = (0, 1, 0, 2, 1, 0)
F32 = jnp.float32
BF16 = jnp.bfloat16
VMEM = pl.BlockSpec(memory_space=pltpu.VMEM)
SMEM = pl.BlockSpec(memory_space=pltpu.SMEM)
ANY = pl.BlockSpec(memory_space=pl.ANY)


def shape(*dims, kind=F32):
    return jax.ShapeDtypeStruct(dims, kind)


def call(kernel, out, in_specs, scratch=(), flops=0, moved=0, room=18):
    return pl.pallas_call(
        kernel,
        out_shape=out,
        in_specs=in_specs,
        out_specs=jax.tree.map(lambda _: VMEM, out),
        scratch_shapes=list(scratch),
        compiler_params=pltpu.CompilerParams(vmem_limit_bytes=room * 2**20),
        cost_estimate=pl.CostEstimate(flops=flops, bytes_accessed=moved, transcendentals=0),
    )


def thirds(value):
    first = value.astype(BF16)
    rest = value - first.astype(F32)
    second = rest.astype(BF16)
    third = (rest - second.astype(F32)).astype(BF16)
    return first, second, third


def pack_kernel(slot_ref, modes_ref, loads_ref, coarse_ref, split_ref, payload_ref, *rest):
    by_slot, parts, (rows, line) = rest[0], rest[1:5], rest[5:]
    by_slot[...] = jnp.zeros_like(by_slot)
    for k in range(2):
        for b in range(SLOTS):
            for i in range(MODES):
                by_slot[k, slot_ref[k, b], i:i + 1] = modes_ref[i, k:k + 1, b * BLK:(b + 1) * BLK]
    for n in range(4):
        parts[n][...] = by_slot[:, 4 + 2 * n:6 + 2 * n]
    rows[...] = jnp.zeros_like(rows)
    rows[0:12] = coarse_ref[...]
    line[...] = jnp.zeros_like(line)
    for k in range(2):
        for i in range(MODES):
            line[k * MODES + i:k * MODES + i + 1] = loads_ref[i, k:k + 1]
    places, tiles = payload_ref.shape[0], rows.shape[1] // BLK
    left = lax.broadcasted_iota(jnp.int32, (MODES, BLK), 1) < 64
    for p in range(places):
        first = (96 * p - 48) % (96 * places)
        tile, shift = first // BLK, first % BLK
        wide = [rows[:, (tile + j) % tiles * BLK:((tile + j) % tiles + 1) * BLK] for j in range(3)]
        window = pltpu.roll(jnp.concatenate(wide, axis=1), 3 * BLK - shift, axis=1)
        tail = window[:, BLK:2 * BLK]
        payload_ref[p, 0:12] = window[0:12, 0:BLK]
        payload_ref[p, 12:18] = jnp.where(left, tail[0:6], pltpu.roll(tail, 64, axis=1)[6:12])
        payload_ref[p, 18:32] = line[0:14]
    for k in range(2):
        for q in range(SLOTS):
            pieces = [piece.astype(F32) for piece in thirds(by_slot[k, q])]
            pieces.append(jnp.zeros_like(pieces[0]))
            split_ref[k, :, q * BLK:(q + 1) * BLK] = jnp.concatenate(pieces, axis=0).astype(BF16)


def pack(slots, modes, loads, coarse_inverse, places):
    return call(
        pack_kernel,
        (shape(2, 32, SLOTS * BLK, kind=BF16), shape(places, 32, BLK), shape(2, SLOTS, 8, BLK))
        + (shape(2, 2, 8, BLK),) * 4,
        [SMEM] + [VMEM] * 3,
        [pltpu.VMEM((ROWS, 96 * places), F32), pltpu.VMEM((ROWS, BLK), F32)],
        room=PACK_ROOM,
    )(slots, modes.transpose(1, 0, 2), loads.transpose(1, 0, 2), coarse_inverse)


def partner(parts, arrived, layout_ref, k, f, c):
    meets = jnp.bitwise_xor(layout_ref[k, f], c)
    if f == 0:
        return parts[0][1 - k, 2 + meets]
    if f == 1:
        return parts[0][1 - k, meets]
    return arrived[f - 2][k, meets]


def own(parts, k, f, c):
    return parts[0][k, 2 * f + c] if f < 2 else parts[f - 1][k, c]


def share(core, table, terms, riders, mine_ref, other_ref, solved):
    result = jnp.dot(table, terms, precision=lax.Precision.HIGHEST, preferred_element_type=F32)
    for n in range(4):
        for x in range(4):
            solved[n, x, 0:12] = result[(4 * n + x) * 12:(4 * n + x + 1) * 12]
    for out_ref, c in ((mine_ref, core), (other_ref, 1 - core)):
        for x in range(4):
            out_ref[x, 0:12] = solved[c + 1, x, 0:12]
            out_ref[x, 12:16] = riders
            out_ref[x, 16:28] = solved[c + 1, max(x - 1, 0), 0:12]
            out_ref[x, 28:40] = solved[c + 1, min(x + 1, 3), 0:12]
            out_ref[x, 40:52] = solved[c, x, 0:12]
            out_ref[x, 52:64] = solved[c + 2, x, 0:12]


def partial_kernel(core_ref, table_ref, terms_ref, *rest):
    mine_ref, other_ref, solved = rest[-3:]
    riders = jnp.sum(terms_ref[:, 8:16], axis=0)[4:8]
    share(core_ref[0], table_ref[...], terms_ref[...].reshape(-1, BLK), riders, mine_ref, other_ref, solved)


def unpack_kernel(core_ref, layout_ref, payload_ref, modes_ref, *rest):
    arrived = rest[0:4]
    table_ref, lift_ref, mine_ref, other_ref, wide, terms, solved = rest[-7:]
    places = payload_ref.shape[0]
    terms[...] = jnp.zeros_like(terms)
    wide[...] = jnp.zeros_like(wide)
    for p in range(places):
        tail = payload_ref[p, 12:18]
        wide[ROWS * p:ROWS * p + 12, 0:BLK] = payload_ref[p, 0:12]
        wide[ROWS * p:ROWS * p + 6, BLK:2 * BLK] = tail
        wide[ROWS * p + 6:ROWS * p + 12, BLK:2 * BLK] = pltpu.roll(tail, 64, axis=1)
        terms[ROWS * p:ROWS * p + 12] = payload_ref[p, 18:30]
    table_ref[...] = wide[...].T[0:192]
    riders = jnp.zeros((4, BLK), F32)
    share(core_ref[0], table_ref[...], terms[...], riders, mine_ref, other_ref, solved)
    lane = lax.broadcasted_iota(jnp.int32, (8, BLK), 1)
    for k in range(2):
        for f in range(6):
            for c in range(2):
                live = lane < layout_ref[k, 6 + 2 * f + c]
                meets = jnp.bitwise_xor(layout_ref[k, f], c)
                theirs = modes_ref[1 - k, 2 * (1 - f) + meets] if f < 2 else arrived[f - 2][k, meets]
                mine = jnp.where(live, modes_ref[k, 2 * f + c], 0.0)
                theirs = jnp.where(live, -theirs, 0.0)
                both = jnp.concatenate([mine[0:MODES], theirs[0:MODES], mine[MODES:8], mine[MODES:8]], axis=0)
                pieces = [piece.astype(F32) for piece in thirds(both)]
                left = jnp.concatenate([pieces[n] for n in SPLIT_LEFT], axis=0)
                lift_ref[k, f, c * BLK:(c + 1) * BLK] = left.T.astype(BF16)


SHARES = (shape(4, 64, BLK), shape(4, 64, BLK))
SOLVED = pltpu.VMEM((4, 4, ROWS, BLK), F32)


def unpack(core, layout, payload, modes, parts, *beside):
    places = payload.shape[0]
    payload = lax.all_to_all(payload, "p", 0, 0, tiled=True)
    return call(
        unpack_kernel,
        (shape(192, places * ROWS), shape(2, 6, 2 * BLK, 6 * ROWS, kind=BF16)) + SHARES,
        [SMEM] * 2 + [VMEM] * (6 + len(beside)),
        [pltpu.VMEM((places * ROWS, 2 * BLK), F32), pltpu.VMEM((places * ROWS, BLK), F32), SOLVED],
    )(core, layout, payload, modes, *send((None, *parts)), *beside)


def collect(mine, other):
    both = mine + lax.ppermute(other, "core", [(0, 1), (1, 0)])
    return lax.all_to_all(both, "x", 0, 0, tiled=True)


def coarse_solve(core, table, terms, *beside):
    gathered = lax.all_to_all(terms, "p", 0, 0, tiled=True)
    specs = [SMEM] + [VMEM] * (2 + len(beside))
    return collect(*call(partial_kernel, SHARES, specs, [SOLVED])(core, table, gathered, *beside))


def load_coefficients(partial_ref, coef_ref):
    solved = jnp.sum(partial_ref[...], axis=0)
    coef_ref[...] = jnp.zeros_like(coef_ref)
    for k in range(2):
        other = MODES * (1 - k)
        firsts = [other, other] + [16 + 12 * n + MODES * k for n in range(4)]
        for f in range(6):
            coef_ref[k, f, 0:MODES] = solved[MODES * k:MODES * (k + 1)]
            coef_ref[k, f, MODES:2 * MODES] = solved[firsts[f]:firsts[f] + MODES]
    return solved[0:16]


def lifted(lift_ref, coef_ref, k, f):
    pieces = thirds(coef_ref[k, f])
    right = jnp.concatenate([pieces[n] for n in SPLIT_RIGHT], axis=0)
    return jnp.dot(lift_ref[k, f], right, preferred_element_type=F32)


def apply_schur(schur_ref, rounded, slot_ref, by_slot, parts, base=None):
    for k in range(2):
        for n in range(3):
            image = jnp.dot(schur_ref[k, n * 512:(n + 1) * 512], rounded[k], preferred_element_type=F32)
            for j in range(4):
                b = 4 * n + j
                piece = image[j * BLK:(j + 1) * BLK]
                if base is not None:
                    piece = base[k, b * BLK:(b + 1) * BLK] - piece
                by_slot[slot_ref[k, b]] = piece
        parts[0][k] = by_slot[0:4]
        for n in range(4):
            parts[n + 1][k] = by_slot[4 + 2 * n:6 + 2 * n]


def round_blocks(field_ref, slot_ref, rounded):
    for k in range(2):
        for b in range(SLOTS):
            rounded[k, b * BLK:(b + 1) * BLK] = field_ref[k, slot_ref[k, b]].astype(BF16)


PARTS = (shape(2, 4, BLK, BLK),) + (shape(2, 2, BLK, BLK),) * 4
FIELD = shape(2, SLOTS, BLK, BLK)
MARK = shape(8, BLK)
SCRATCH = [
    pltpu.VMEM((2, 6, ROWS, BLK), F32),
    pltpu.VMEM((2, SLOTS * BLK, BLK), BF16),
    pltpu.VMEM((SLOTS, BLK, BLK), F32),
]


def first_kernel(slot_ref, partial_ref, lift_ref, schur_ref, gap_ref, *rest):
    images = rest[0:5]
    coef_ref, rounded, by_slot, field_ref = rest[5:]
    load_coefficients(partial_ref, coef_ref)
    for k in range(2):
        for f in range(6):
            field_ref[k, 2 * f:2 * f + 2] = lifted(lift_ref, coef_ref, k, f).reshape(2, BLK, BLK)
    round_blocks(field_ref, slot_ref, rounded)
    apply_schur(schur_ref, rounded, slot_ref, by_slot, images, gap_ref)


def project_kernel(slot_ref, partial_ref, lift_ref, schur_ref, residual_ref, *rest):
    field_ref, images = rest[0], rest[1:6]
    coef_ref, rounded, by_slot = rest[6:]
    load_coefficients(partial_ref, coef_ref)
    for k in range(2):
        for f in range(6):
            lift = lifted(lift_ref, coef_ref, k, f).reshape(2, BLK, BLK)
            field_ref[k, 2 * f:2 * f + 2] = residual_ref[k, 2 * f:2 * f + 2] - lift
    round_blocks(field_ref, slot_ref, rounded)
    apply_schur(schur_ref, rounded, slot_ref, by_slot, images)


def step_kernel(slot_ref, partial_ref, lift_ref, schur_ref, image_ref, projected_ref, *rest):
    sums_ref, change_ref, field_ref, images = rest[0], rest[1], rest[2], rest[3:8]
    coef_ref, rounded, by_slot = rest[8:]
    sums = load_coefficients(partial_ref, coef_ref)[8:16]
    sums_ref[...] = sums
    alpha = sums[4:5] / sums[5:6]
    for k in range(2):
        for f in range(6):
            pair = slice(2 * f, 2 * f + 2)
            change = image_ref[k, pair] - lifted(lift_ref, coef_ref, k, f).reshape(2, BLK, BLK)
            change_ref[k, pair] = change
            field_ref[k, pair] = projected_ref[k, pair] - alpha[None] * change
    round_blocks(field_ref, slot_ref, rounded)
    apply_schur(schur_ref, rounded, slot_ref, by_slot, images)


def last_kernel(
    partial_ref, lift_ref, sums_ref, change_ref, second_ref, image_ref, norm_ref, scale_ref, coef_ref
):
    riders = load_coefficients(partial_ref, coef_ref)
    start_norm, start_curve = sums_ref[4:5], sums_ref[5:6]
    norm, second_curve, cross, back = riders[12:13], riders[13:14], riders[14:15], riders[15:16]
    beta = norm / start_norm
    curve = second_curve + beta * (cross + back) + beta * beta * start_curve
    step = norm / curve
    scale_ref[...] = jnp.zeros_like(scale_ref)
    scale_ref[0:1] = start_norm / start_curve
    scale_ref[1:2] = beta
    scale_ref[2:3] = step
    total = jnp.zeros((8, BLK), F32)
    for k in range(2):
        for f in range(6):
            pair = slice(2 * f, 2 * f + 2)
            lift = lifted(lift_ref, coef_ref, k, f).reshape(2, BLK, BLK)
            change = (image_ref[k, pair] - lift) + beta[None] * change_ref[k, pair]
            left = second_ref[k, pair] - step[None] * change
            total = total + jnp.sum((left * left).reshape(-1, 8, BLK), axis=0)
    norm_ref[...] = jnp.broadcast_to(jnp.sum(total, axis=0, keepdims=True)[None], norm_ref.shape)


def total_kernel(norm_ref, beside_ref, total_ref):
    total_ref[...] = jnp.sum(norm_ref[...], axis=0)


def multipliers_kernel(
    slot_ref, scale_ref, partial_ref, lift_ref, first_ref, second_ref, multipliers_ref, mark_ref, coef_ref, by_slot
):
    load_coefficients(partial_ref, coef_ref)
    alpha, beta, step = scale_ref[0:1], scale_ref[1:2], scale_ref[2:3]
    for k in range(2):
        for f in range(6):
            pair = slice(2 * f, 2 * f + 2)
            start = lifted(lift_ref, coef_ref, k, f).reshape(2, BLK, BLK)
            first = first_ref[k, pair]
            direction = second_ref[k, pair] + beta[None] * first
            by_slot[pair] = (start + alpha[None] * first) + step[None] * direction
        for b in range(SLOTS):
            multipliers_ref[k, b * BLK:(b + 1) * BLK] = by_slot[slot_ref[k, b]]
    mark_ref[...] = jnp.zeros_like(mark_ref)


def combine_kernel(dots, layout_ref, split_ref, *rest):
    parts, arrived = rest[0:5], rest[5:9]
    extras, (field_ref, terms_ref, line_ref) = rest[9:-3], rest[-3:]
    row = lax.broadcasted_iota(jnp.int32, (BLK, BLK), 0)
    line_ref[...] = jnp.zeros_like(line_ref)
    totals = [jnp.zeros((8, BLK), F32) for _ in dots]
    for k in range(2):
        for f in range(6):
            for c in range(2):
                q = 2 * f + c
                gap = own(parts, k, f, c) - partner(parts, arrived, layout_ref, k, f, c)
                block = jnp.where(row < layout_ref[k, 6 + q], gap, 0.0)
                field_ref[k, q] = block
                for n, (left, right) in enumerate(dots):
                    a = block if left is None else extras[left][k, q]
                    b = block if right is None else extras[right][k, q]
                    totals[n] = totals[n] + jnp.sum((a * b).reshape(BLK // 8, 8, BLK), axis=0)
        pieces = thirds(field_ref[k].reshape(SLOTS * BLK, BLK))
        one = jnp.dot(split_ref[k], pieces[0], preferred_element_type=F32)
        two = jnp.dot(split_ref[k], pieces[1], preferred_element_type=F32)
        three = jnp.dot(split_ref[k], pieces[2], preferred_element_type=F32)
        terms = one[0:8] + ((one[8:16] + two[0:8]) + ((one[16:24] + two[8:16]) + three[0:8]))
        line_ref[MODES * k:MODES * (k + 1)] = terms[0:MODES]
    for n, total in enumerate(totals):
        line_ref[12 + n:13 + n] = jnp.sum(total, axis=0, keepdims=True)
    terms_ref[...] = jnp.broadcast_to(line_ref[...][None], terms_ref.shape)


def send(parts):
    def moved(value, axis, step):
        count = lax.axis_size(axis)
        return lax.ppermute(value, axis, [(i, (i + step) % count) for i in range(count)])

    sub = ("p", "core")
    return (
        moved(parts[2], "x", 1), moved(parts[1], "x", -1),
        moved(parts[4], sub, 1), moved(parts[3], sub, -1),
    )


def combine(dots, places, layout, split, parts, *extras):
    kernel = functools.partial(combine_kernel, dots)
    out = (FIELD, shape(places, ROWS, BLK))
    specs = [SMEM] + [VMEM] * (10 + len(extras))
    return call(kernel, out, specs, [pltpu.VMEM((ROWS, BLK), F32)])(
        layout, split, *parts, *send(parts), *extras
    )


def body(schur, local_gap, modes, rigid_loads, coarse_inverse, slots, swaps, lengths):
    places = lax.axis_size("p")
    core = jnp.full((1,), lax.axis_index("core"), jnp.int32)
    operator_flops = 2 * 2 * SLOTS * BLK * SLOTS * BLK * BLK
    operator_bytes = 2 * SLOTS * BLK * SLOTS * BLK * 2

    layout = jnp.concatenate([swaps, lengths], axis=1)
    split, payload, own_modes, *mode_parts = pack(slots, modes, rigid_loads, coarse_inverse, places)
    table, lift, *shares = unpack(core, layout, payload, own_modes, mode_parts)
    started = collect(*shares)
    images = call(
        first_kernel, PARTS, [SMEM] + [VMEM] * 4, SCRATCH + [pltpu.VMEM((2, SLOTS, BLK, BLK), F32)],
        operator_flops, operator_bytes,
    )(slots, started, lift, schur, local_gap)
    residual, terms = combine((), places, layout, split, images)

    partial = coarse_solve(core, table, terms, schur)
    projected, *images = call(
        project_kernel, (FIELD,) + PARTS, [SMEM] + [VMEM] * 4, SCRATCH, operator_flops, operator_bytes
    )(slots, partial, lift, schur, residual)
    image, terms = combine(((0, 0), (0, None)), places, layout, split, images, projected)

    partial = coarse_solve(core, table, terms, schur)
    sums, change, second, *images = call(
        step_kernel, (shape(8, BLK), FIELD, FIELD) + PARTS, [SMEM] + [VMEM] * 5,
        SCRATCH, operator_flops, operator_bytes,
    )(slots, partial, lift, schur, image, projected)
    dots = ((0, 0), (0, None), (1, None), (0, 2))
    second_image, terms = combine(dots, places, layout, split, images, second, projected, image)

    partial = coarse_solve(core, table, terms)
    norm, scale = call(
        last_kernel, (shape(places, NORM_ROWS, BLK), shape(8, BLK)), [VMEM] * 6, [SCRATCH[0]]
    )(partial, lift, sums, change, second, second_image)
    norm = lax.all_to_all(norm, "p", 0, 0, tiled=True)
    multipliers, mark = call(
        multipliers_kernel, (shape(2, SLOTS * BLK, BLK), MARK), [SMEM] + [VMEM] * 5, [SCRATCH[0], SCRATCH[2]], room=60
    )(slots, scale, started, lift, projected, second)
    norm = call(total_kernel, shape(NORM_ROWS, BLK), [VMEM, ANY])(norm, mark)
    norm = norm + lax.ppermute(norm, "core", [(0, 1), (1, 0)])
    norm = lax.all_to_all(jnp.broadcast_to(norm[None], (4, NORM_ROWS, BLK)), "x", 0, 0, tiled=True)
    return multipliers, jnp.sqrt(jnp.sum(norm[:, 0], axis=0) / sums[4])


def solution(mesh):
    fine = Mesh(mesh.devices.reshape(-1, 2, 4), ("p", "core", "x"))
    everywhere = ("p", "core", "x")
    deep, flat = P(everywhere, None, None), P(everywhere, None)
    in_specs = (deep, deep, deep, deep, flat, flat, flat, flat)
    return jax.shard_map(body, mesh=fine, in_specs=in_specs, out_specs=(deep, P()), check_vma=False)
```
